32 devices in a mesh: groups: 2 (over x), seq: 16 (over z, y, core).
Axes of the slice: x: 2, y: 2, z: 4, core: 2. Of those that a mesh axis runs over, the one named last changes fastest.
Arguments:
- hidden: bfloat16 [4096, 4608], P(('groups', 'seq')), parts along dimension 0, may hold values from -6 to 6
- packed_weight_codes: int32 [1152, 2048], replicated, may hold values from 0 to 65535
- block_scale_codes: int32 [72, 2048], replicated, may hold values from 0 to 255
- grouped_scale: float32 [72, 8], replicated, may hold values from 0.06 to 0.18
- adapter_down_weight: float32 [128, 4608], replicated, may hold values from -0.09375 to 0.09375
- key_up_weight: float32 [64, 1024], replicated, may hold values from -0.75 to 0.75
- value_up_weight: float32 [64, 1024], replicated, may hold values from -0.75 to 0.75
- queries: bfloat16 [4096, 2048], P(('groups', 'seq')), parts along dimension 0, may hold values from -6 to 6
- chosen_output_gradient: bfloat16 [4096, 2048], P(('groups', 'seq')), parts along dimension 0, may hold values from -6 to 6
- rejected_output_gradient: bfloat16 [4096, 2048], P(('groups', 'seq')), parts along dimension 0, may hold values from -6 to 6
- sequence_log_likelihoods: float32 [8], P('groups'), parts along dimension 0, may hold values from -42 to -40
- lengths: int32 [6], P('groups'), parts along dimension 0, may hold values from 64 to 1536, as said below
Outputs:
- attention_output: bfloat16 [4096, 2048], P(('groups', 'seq')), parts along dimension 0
- query_gradient: bfloat16 [4096, 2048], P(('groups', 'seq')), parts along dimension 0
- hidden_gradient: bfloat16 [4096, 4608], P(('groups', 'seq')), parts along dimension 0
- adapter_down_gradient: float32 [256, 4608], P('groups'), parts along dimension 0
- key_adapter_gradient: float32 [128, 1024], P('groups'), parts along dimension 0
- value_adapter_gradient: float32 [128, 1024], P('groups'), parts along dimension 0
The draws below stay inside these ranges and needn't reach their ends.
There are 2 independent parts, one for each index of `groups`. The reference program is written for one: setup_inputs(seed, part) draws one part's arguments, and reference() takes and returns one part's arrays. A program takes and returns all parts, laid end to end along the dimension named above; an argument that names none is the same for every part. Nothing has to cross between parts.
Inputs may be any that keep to these rules, and one draw needn't show every extreme that they name: `packed_weight_codes`: each word holds four 4-bit codes, the k-th (k = 0 to 3, lowest bits first) for input row 4 r + k of packed row r. lengths[0] is the prompt's length, 768 or more; lengths[1] and lengths[2] are the responses' lengths, 64 or more, and one of the two equals 256.
All inputs are finite; a program needn't handle non-finite values.
Results may differ from the reference program's by a relative error of at most 0.018.
The reference program's roundings to bfloat16 on the way count: a program that leaves them out, or rounds other values in their place, can miss the bound.
Values may be sent and summed in bfloat16 or wider, within the bound.
A program may use at most 256 MiB of HBM per device.

```python
import math
import jax
import jax.numpy as jnp
from jax import lax

MODEL_WIDTH = 4608
HEADS = 16
KEY_VALUE_HEADS = 8
HEAD_DIMENSION = 128
ADAPTER_RANK = 64
BLOCK = 64
GROUP = 256
TOK_DEV = 128
TOKENS = 2048
PROMPT = 1536
RESP = 256
N_SEQ = 16


def draw_lengths(key, part):
    key = jax.random.fold_in(key, 7)
    prompt_key, short_key, pick_key = jax.random.split(key, 3)
    prompt_length = jax.random.randint(prompt_key, (), PROMPT // 2, PROMPT + 1)
    short_length = jax.random.randint(short_key, (), RESP // 4, RESP + 1)
    chosen_long = jax.random.randint(pick_key, (), 0, 2)
    chosen_length = jnp.where(chosen_long == 1, RESP, short_length)
    rejected_length = jnp.where(chosen_long == 1, short_length, RESP)
    return jnp.stack([prompt_length, chosen_length, rejected_length]).astype(jnp.int32)


def with_ends(array, key, least, largest):
    longest = array.shape.index(max(array.shape))
    spots = []
    for shift in (0, 1):
        where = [jax.random.randint(jax.random.fold_in(key, axis), (), 0, length) for axis, length in enumerate(array.shape)]
        where[longest] = (where[longest] + shift) % array.shape[longest]
        spots.append(tuple(where))
    return array.at[spots[0]].set(least).at[spots[1]].set(largest)


def level_of(stream_key, shape, cuts, least, top_value):
    factor_of = 1.0
    for axis_at, blocks in cuts:
        draws = jax.random.uniform(jax.random.fold_in(jax.random.fold_in(stream_key, 6), axis_at), (blocks,), jnp.float32, least / len(cuts), top_value / len(cuts))
        factor_of = factor_of * jnp.repeat(jnp.exp(draws), shape[axis_at] // blocks).reshape((-1,) + (1,) * (len(shape) - 1 - axis_at))
    return factor_of


def noise(own_key, extent, scale, bound, shards=(), kind=jnp.bfloat16):
    drawn = jax.random.normal(own_key, extent, jnp.float32) * scale
    if len(shards) > 0:
        drawn = level_of(own_key, extent, shards, -0.22, 0.18) * drawn
    return jnp.clip(drawn, min=-bound, max=bound).astype(kind)


def setup_inputs(seed: int = 0, part: int = 0) -> dict:
    seeds = jax.random.split(jax.random.key(seed), 13)
    part_keys = jax.random.split(jax.random.fold_in(seeds[12], part), 13)
    hidden = noise(part_keys[0], (TOKENS, MODEL_WIDTH), 1.0, 6.0, ((0, 16),))
    packed_weight_codes = with_ends(jax.random.randint(seeds[1], (MODEL_WIDTH // 4, 2 * KEY_VALUE_HEADS * HEAD_DIMENSION), 0, 65536), jax.random.fold_in(seeds[1], 1), 0, 65535).astype(jnp.int32)
    block_scale_codes = with_ends(jax.random.randint(seeds[2], (MODEL_WIDTH // BLOCK, 2 * KEY_VALUE_HEADS * HEAD_DIMENSION), 0, 256), jax.random.fold_in(seeds[2], 1), 0, 255).astype(jnp.int32)
    grouped_scale = jnp.clip(jnp.exp(jax.random.uniform(seeds[3], (MODEL_WIDTH // BLOCK, 2 * KEY_VALUE_HEADS * HEAD_DIMENSION // GROUP), jnp.float32, math.log(0.06), math.log(0.18))), 0.06, 0.18)
    adapter_down_weight = noise(seeds[4], (2 * ADAPTER_RANK, MODEL_WIDTH), MODEL_WIDTH ** -0.5, 0.09375, (), jnp.float32)
    key_up_weight = noise(seeds[5], (ADAPTER_RANK, KEY_VALUE_HEADS * HEAD_DIMENSION), ADAPTER_RANK ** -0.5, 0.75, (), jnp.float32)
    value_up_weight = noise(seeds[6], (ADAPTER_RANK, KEY_VALUE_HEADS * HEAD_DIMENSION), ADAPTER_RANK ** -0.5, 0.75, (), jnp.float32)
    queries = noise(part_keys[7], (TOKENS, HEADS * HEAD_DIMENSION), 1.0, 6.0, ((0, 16),))
    chosen_output_gradient = noise(part_keys[8], (TOKENS, HEADS * HEAD_DIMENSION), 1.0, 6.0, ((0, 16),))
    rejected_output_gradient = noise(part_keys[9], (TOKENS, HEADS * HEAD_DIMENSION), 1.0, 6.0, ((0, 16),))
    sequence_log_likelihoods = jnp.clip(jax.random.uniform(part_keys[10], (4,), jnp.float32, -42.0, -40.0), -42.0, -40.0)
    lengths = draw_lengths(jax.random.fold_in(jax.random.fold_in(seeds[12], part), 71), part)
    return dict(hidden=hidden, packed_weight_codes=packed_weight_codes, block_scale_codes=block_scale_codes, grouped_scale=grouped_scale, adapter_down_weight=adapter_down_weight, key_up_weight=key_up_weight, value_up_weight=value_up_weight, queries=queries, chosen_output_gradient=chosen_output_gradient, rejected_output_gradient=rejected_output_gradient, sequence_log_likelihoods=sequence_log_likelihoods, lengths=lengths)


nf4_levels = (-1.0, -0.6961928009986877, -0.5250730514526367, -0.39491748809814453, -0.28444138169288635, -0.18477343022823334, -0.09105003625154495, 0.0, 0.07958029955625534, 0.16093020141124725, 0.24611230194568634, 0.33791524171829224, 0.44070982933044434, 0.5626170039176941, 0.7229568362236023, 1.0)
score_scale = 1.0 / 12.0
soft_cap = 50.0
dpo_beta = 0.5
adapter_multiplier = 0.5
rope_base = 10000.0


def dequantize(packed_weight_codes, block_scale_codes, grouped_scale):
    packed_rows, columns = packed_weight_codes.shape
    nibbles = jnp.stack([jnp.bitwise_and(jnp.right_shift(packed_weight_codes, 4 * shift_count), 15) for shift_count in range(4)], axis=1)
    levels = jnp.zeros(nibbles.shape, jnp.float32)
    for level_index in range(16):
        levels = jnp.where(nibbles == level_index, jnp.float32(nf4_levels[level_index]), levels)
    block_rows = block_scale_codes.shape[0]
    group_count = grouped_scale.shape[1]
    spread = jnp.broadcast_to(grouped_scale[:, :, None], (block_rows, group_count, columns // group_count)).reshape(block_rows, columns)
    absmax = spread * (block_scale_codes.astype(jnp.float32) + 1.0) / 256.0
    scaled = levels.reshape(block_rows, -1, columns) * absmax[:, None, :]
    return scaled.reshape(packed_rows * 4, columns).astype(jnp.bfloat16)


def row_info(rows, lengths, prompt_rows, reply_rows):
    segment = jnp.where(rows < prompt_rows, 0, jnp.where(rows < prompt_rows + reply_rows, 1, 2)).astype(jnp.int32)
    offset = rows - jnp.where(segment == 0, 0, jnp.where(segment == 1, prompt_rows, prompt_rows + reply_rows)).astype(jnp.int32)
    limit = jnp.where(segment == 0, lengths[0], jnp.where(segment == 1, lengths[1], lengths[2]))
    valid = offset < limit
    position = jnp.where(segment == 0, offset, lengths[0] + offset).astype(jnp.int32)
    return segment, valid, position


def rope_tables(position, head_size):
    half_size = head_size // 2
    inverse = rope_base ** (-2.0 * jnp.arange(half_size, dtype=jnp.float32) / head_size)
    angles = position.astype(jnp.float32)[:, None] * inverse[None, :]
    return jnp.cos(angles), jnp.sin(angles)


def rotate(values, cosine, sine, head_size, direction):
    count = values.shape[0]
    shaped = values.reshape(count, -1, 2, head_size // 2)
    first = shaped[:, :, 0]
    second = shaped[:, :, 1]
    cos_rows = cosine[:, None, :]
    sin_rows = direction * sine[:, None, :]
    turned = jnp.stack([first * cos_rows - second * sin_rows, second * cos_rows + first * sin_rows], axis=2)
    return turned.reshape(count, -1)


def allowed_pairs(query_rows, query_info, key_rows, key_info):
    same = (key_info[0][None, :] == 0) | (key_info[0][None, :] == query_info[0][:, None])
    both = query_info[1][:, None] & key_info[1][None, :]
    return same & both & (key_rows[None, :] <= query_rows[:, None])


def capped_scores(grouped, key_heads):
    raw = jnp.einsum("rkgd,tkd->kgrt", grouped, key_heads) * score_scale
    return soft_cap * jnp.tanh(raw / soft_cap)


def rounded(values):
    return lax.optimization_barrier(values.astype(jnp.bfloat16)).astype(jnp.float32)


def reference(hidden, packed_weight_codes, block_scale_codes, grouped_scale, adapter_down_weight, key_up_weight, value_up_weight, queries, chosen_output_gradient, rejected_output_gradient, sequence_log_likelihoods, lengths):
    key_feature_width = KEY_VALUE_HEADS * HEAD_DIMENSION
    group_size = HEADS // KEY_VALUE_HEADS
    all_rows = jnp.arange(TOKENS, dtype=jnp.int32)
    info = row_info(all_rows, lengths, PROMPT, RESP)
    cosine, sine = rope_tables(info[2], HEAD_DIMENSION)
    weight = dequantize(packed_weight_codes, block_scale_codes, grouped_scale)
    down_projection_half = adapter_down_weight.astype(jnp.bfloat16)
    key_lowrank_update = key_up_weight.astype(jnp.bfloat16)
    value_lowrank_update = value_up_weight.astype(jnp.bfloat16)
    base = jnp.dot(hidden, weight, preferred_element_type=jnp.float32)
    reduced_rank_state = lax.dot_general(hidden, down_projection_half, (((1,), (1,)), ((), ())), preferred_element_type=jnp.float32).astype(jnp.bfloat16)
    key_linear = base[:, :key_feature_width] + adapter_multiplier * jnp.dot(reduced_rank_state[:, :ADAPTER_RANK], key_lowrank_update, preferred_element_type=jnp.float32)
    values = (base[:, key_feature_width:] + adapter_multiplier * jnp.dot(reduced_rank_state[:, ADAPTER_RANK:], value_lowrank_update, preferred_element_type=jnp.float32)).astype(jnp.bfloat16)
    keys = rotate(key_linear, cosine, sine, HEAD_DIMENSION, 1.0).astype(jnp.bfloat16)
    key_heads = keys.reshape(TOKENS, KEY_VALUE_HEADS, HEAD_DIMENSION).astype(jnp.float32)
    value_heads = values.reshape(TOKENS, KEY_VALUE_HEADS, HEAD_DIMENSION).astype(jnp.float32)
    block_shape = (N_SEQ, TOK_DEV, KEY_VALUE_HEADS, group_size, HEAD_DIMENSION)
    query_blocks = queries.reshape(block_shape)
    row_blocks = all_rows.reshape(N_SEQ, TOK_DEV)

    def block_setup(rows_block):
        block_info = row_info(rows_block, lengths, PROMPT, RESP)
        return block_info, allowed_pairs(rows_block, block_info, all_rows, info)

    def forward_one(inputs):
        query_block, rows_block = inputs
        block_info, allowed = block_setup(rows_block)
        capped = capped_scores(query_block.astype(jnp.float32), key_heads)
        weights = jnp.where(allowed[None, None], jnp.exp(capped), 0.0)
        numerator = jnp.einsum("kgrt,tkd->rkgd", rounded(weights), value_heads)
        denominator = jnp.sum(weights, axis=3) + (1.0 - block_info[1].astype(jnp.float32))[None, None, :]
        output = numerator / jnp.transpose(denominator, (2, 0, 1))[..., None]
        return output.astype(jnp.bfloat16), denominator

    out_blocks, denominators = lax.map(forward_one, (query_blocks, row_blocks))
    margin = dpo_beta * ((sequence_log_likelihoods[0] - sequence_log_likelihoods[2]) - (sequence_log_likelihoods[1] - sequence_log_likelihoods[3]))
    pair_weight = dpo_beta * jax.nn.sigmoid(-margin)

    def backward_one(carry, inputs):
        query_block, rows_block, out_block, denominator, chosen_block, rejected_block = inputs
        block_info, allowed = block_setup(rows_block)
        in_chosen = (block_info[0] != 2).astype(jnp.float32)[:, None, None, None]
        in_rejected = (block_info[0] != 1).astype(jnp.float32)[:, None, None, None]
        grad_out = (pair_weight * (rejected_block.astype(jnp.float32) * in_rejected - chosen_block.astype(jnp.float32) * in_chosen)).astype(jnp.bfloat16)
        grad_float = grad_out.astype(jnp.float32)
        delta = jnp.transpose(jnp.sum(grad_float * out_block.astype(jnp.float32), axis=3), (1, 2, 0))
        query_float = query_block.astype(jnp.float32)
        capped = capped_scores(query_float, key_heads)
        prob = jnp.where(allowed[None, None], jnp.exp(capped), 0.0) / denominator[..., None]
        dprob = jnp.einsum("rkgd,tkd->kgrt", grad_float, value_heads)
        slope = rounded(prob * (dprob - delta[..., None]) * (1.0 - (capped / soft_cap) ** 2) * score_scale)
        query_grad = jnp.einsum("kgrt,tkd->rkgd", slope, key_heads)
        key_term = jnp.einsum("kgrt,rkgd->tkd", slope, query_float).reshape(TOKENS, -1)
        value_term = jnp.einsum("kgrt,rkgd->tkd", rounded(prob), grad_float).reshape(TOKENS, -1)
        term = jnp.concatenate([key_term, value_term], axis=1)
        return carry + term, query_grad.astype(jnp.bfloat16)

    summed, query_grads = lax.scan(backward_one, jnp.zeros((TOKENS, 2 * key_feature_width), jnp.float32), (query_blocks, row_blocks, out_blocks, denominators, chosen_output_gradient.reshape(block_shape), rejected_output_gradient.reshape(block_shape)))
    attention_output = out_blocks.reshape(TOKENS, -1)
    query_gradient = query_grads.reshape(TOKENS, -1)
    key_grad = rotate(summed[:, :key_feature_width], cosine, sine, HEAD_DIMENSION, -1.0)
    projection_gradient = jnp.concatenate([key_grad, summed[:, key_feature_width:]], axis=1).astype(jnp.bfloat16)
    contracted_rows = (((0,), (0,)), ((), ()))
    key_adapter_gradient = adapter_multiplier * lax.dot_general(reduced_rank_state[:, :ADAPTER_RANK], projection_gradient[:, :key_feature_width], contracted_rows, preferred_element_type=jnp.float32)
    value_adapter_gradient = adapter_multiplier * lax.dot_general(reduced_rank_state[:, ADAPTER_RANK:], projection_gradient[:, key_feature_width:], contracted_rows, preferred_element_type=jnp.float32)
    contract_cols = (((1,), (1,)), ((), ()))
    reduced_rank_gradient = (adapter_multiplier * jnp.concatenate([lax.dot_general(projection_gradient[:, :key_feature_width], key_lowrank_update, contract_cols, preferred_element_type=jnp.float32), lax.dot_general(projection_gradient[:, key_feature_width:], value_lowrank_update, contract_cols, preferred_element_type=jnp.float32)], axis=1)).astype(jnp.bfloat16)
    adapter_down_gradient = lax.dot_general(reduced_rank_gradient, hidden, contracted_rows, preferred_element_type=jnp.float32)
    hidden_gradient = (lax.dot_general(projection_gradient, weight, contract_cols, preferred_element_type=jnp.float32) + jnp.dot(reduced_rank_gradient, down_projection_half, preferred_element_type=jnp.float32)).astype(jnp.bfloat16)
    return (attention_output, query_gradient, hidden_gradient, adapter_down_gradient, key_adapter_gradient, value_adapter_gradient)
```

```python
import functools

import jax
import jax.numpy as jnp
from jax import lax
from jax.experimental import pallas as pl
from jax.experimental.pallas import tpu as pltpu
from jax.sharding import PartitionSpec as P

HEADS = 16
KEY_VALUE_HEADS = 8
HEAD_DIMENSION = 128
ADAPTER_RANK = 64
CHUNK = 128
BLOCK_Q = 256
BLOCK_K = 256

nf4_levels = (
    -1.0,
    -0.6961928009986877,
    -0.5250730514526367,
    -0.39491748809814453,
    -0.28444138169288635,
    -0.18477343022823334,
    -0.09105003625154495,
    0.0,
    0.07958029955625534,
    0.16093020141124725,
    0.24611230194568634,
    0.33791524171829224,
    0.44070982933044434,
    0.5626170039176941,
    0.7229568362236023,
    1.0,
)
score_scale = 1.0 / 12.0
soft_cap = 50.0
dpo_beta = 0.5
adapter_multiplier = 0.5
rope_base = 10000.0

NT = (((1,), (1,)), ((), ()))
NN = (((1,), (0,)), ((), ()))


def dot(a, b, dims=NN):
    return lax.dot_general(a, b, dims, preferred_element_type=jnp.float32)


def project_kernel(
    hidden_ref,
    codes_ref,
    absmax_ref,
    table_ref,
    perm_ref,
    down_ref,
    key_up_ref,
    value_up_ref,
    cos_ref,
    sin_ref,
    weight_ref,
    hidden_t_ref,
    kv_ref,
    low_ref,
    acc,
    low_acc,
):
    step = pl.program_id(0)

    @pl.when(step == 0)
    def _():
        acc[...] = jnp.zeros_like(acc)
        low_acc[...] = jnp.zeros_like(low_acc)

    hidden = hidden_ref[...]
    hidden_t_ref[...] = jnp.transpose(hidden.astype(jnp.float32)).astype(jnp.bfloat16)
    permuted = dot(hidden, perm_ref[...]).astype(jnp.bfloat16)
    low_acc[...] += dot(hidden, down_ref[...].astype(jnp.bfloat16), NT)
    rows, columns = codes_ref.shape
    blocks = absmax_ref.shape[0]
    table = table_ref[...]
    for column in range(0, columns, 128):
        span = slice(column, column + 128)
        scale = jnp.broadcast_to(
            absmax_ref[:, span][:, None, :], (blocks, rows // blocks, 128)
        ).reshape(rows, 128)
        codes = codes_ref[:, span]
        for nibble in range(4):
            index = lax.bitwise_and(lax.shift_right_logical(codes, 4 * nibble), 15)
            level = jnp.take_along_axis(table, index, axis=1, mode="promise_in_bounds")
            weight_ref[nibble * rows : (nibble + 1) * rows, span] = (level * scale).astype(
                jnp.bfloat16
            )
    acc[...] += dot(permuted, weight_ref[...])

    @pl.when(step == pl.num_programs(0) - 1)
    def _():
        low = low_acc[...].astype(jnp.bfloat16)
        low_ref[...] = low
        key_add = adapter_multiplier * dot(
            low[:, :ADAPTER_RANK], key_up_ref[...].astype(jnp.bfloat16)
        )
        value_add = adapter_multiplier * dot(
            low[:, ADAPTER_RANK:], value_up_ref[...].astype(jnp.bfloat16)
        )
        cosine = cos_ref[...]
        sine = sin_ref[...]
        width = KEY_VALUE_HEADS * HEAD_DIMENSION
        for head in range(KEY_VALUE_HEADS):
            span = slice(head * HEAD_DIMENSION, (head + 1) * HEAD_DIMENSION)
            linear = acc[:, span] + key_add[:, span]
            turned = linear * cosine + pltpu.roll(linear, HEAD_DIMENSION // 2, 1) * sine
            kv_ref[2 * head] = turned.astype(jnp.bfloat16)
            kv_ref[2 * head + 1] = (
                acc[:, width + head * HEAD_DIMENSION : width + (head + 1) * HEAD_DIMENSION]
                + value_add[:, span]
            ).astype(jnp.bfloat16)


def project(hidden, codes, absmax, table, perm, down, key_up, value_up, cosine, sine):
    rows, width = hidden.shape
    columns = codes.shape[1]
    steps = codes.shape[0] // CHUNK
    blocks = absmax.shape[0] // steps
    whole = lambda array: pl.BlockSpec(array.shape, lambda i: (0,) * array.ndim)
    return pl.pallas_call(
        project_kernel,
        grid=(steps,),
        in_specs=[
            pl.BlockSpec((rows, 4 * CHUNK), lambda i: (0, i)),
            pl.BlockSpec((CHUNK, columns), lambda i: (i, 0)),
            pl.BlockSpec((blocks, columns), lambda i: (i, 0)),
            whole(table),
            whole(perm),
            pl.BlockSpec((2 * ADAPTER_RANK, 4 * CHUNK), lambda i: (0, i)),
            whole(key_up),
            whole(value_up),
            whole(cosine),
            whole(sine),
        ],
        out_specs=[
            pl.BlockSpec((4 * CHUNK, columns), lambda i: (i, 0)),
            pl.BlockSpec((4 * CHUNK, rows), lambda i: (i, 0)),
            pl.BlockSpec((2 * KEY_VALUE_HEADS, rows, HEAD_DIMENSION), lambda i: (0, 0, 0)),
            pl.BlockSpec((rows, 2 * ADAPTER_RANK), lambda i: (0, 0)),
        ],
        out_shape=[
            jax.ShapeDtypeStruct((width, columns), jnp.bfloat16),
            jax.ShapeDtypeStruct((width, rows), jnp.bfloat16),
            jax.ShapeDtypeStruct((2 * KEY_VALUE_HEADS, rows, HEAD_DIMENSION), jnp.bfloat16),
            jax.ShapeDtypeStruct((rows, 2 * ADAPTER_RANK), jnp.bfloat16),
        ],
        scratch_shapes=[
            pltpu.VMEM((rows, columns), jnp.float32),
            pltpu.VMEM((rows, 2 * ADAPTER_RANK), jnp.float32),
        ],
        compiler_params=pltpu.CompilerParams(vmem_limit_bytes=40 * 1024 * 1024),
        cost_estimate=pl.CostEstimate(
            flops=2 * rows * width * columns + 40 * width * columns,
            bytes_accessed=4 * codes.size + 2 * width * columns,
            transcendentals=0,
        ),
    )(hidden, codes, absmax, table, perm, down, key_up, value_up, cosine, sine)


def attention_kernel(
    parts,
    row_block,
    scalars,
    qg_ref,
    own_ref,
    other_ref,
    back_ref,
    keep_ref,
    send_ref,
    keys,
    values,
    keys_t,
    values_t,
    key_grad,
    value_grad,
    cap_scr,
    weight_scr,
):
    step = pl.program_id(0)
    token_count = keys.shape[0]
    prompt_rows = 3 * token_count // 4
    reply_rows = token_count // 8
    sub_rows = row_block // parts
    even = scalars[3] == 0
    prompt_length = scalars[0]

    @pl.when(step == 0)
    def _():
        own = own_ref[...]
        other = other_ref[...]
        key = jnp.where(even, own.astype(jnp.float32), other.astype(jnp.float32))
        value = jnp.where(even, other.astype(jnp.float32), own.astype(jnp.float32))
        keys[...] = key.astype(jnp.bfloat16)
        values[...] = value.astype(jnp.bfloat16)
        keys_t[...] = jnp.transpose(key).astype(jnp.bfloat16)
        values_t[...] = jnp.transpose(value).astype(jnp.bfloat16)
        key_grad[...] = jnp.zeros_like(key_grad)
        value_grad[...] = jnp.zeros_like(value_grad)

    count = BLOCK_Q // sub_rows
    query = jnp.concatenate([qg_ref[s, :sub_rows] for s in range(count)], axis=0)
    grad = jnp.concatenate([qg_ref[s, sub_rows:] for s in range(count)], axis=0)

    lane = lax.broadcasted_iota(jnp.int32, (1, BLOCK_Q), 1)
    span = BLOCK_Q * parts
    first_row = step * span
    query_row = first_row + (lane // sub_rows) * row_block + scalars[4] * sub_rows + lane % sub_rows
    in_prompt = first_row < prompt_rows
    in_chosen = first_row < prompt_rows + reply_rows
    segment_start = jnp.where(
        in_prompt, 0, jnp.where(in_chosen, prompt_rows, prompt_rows + reply_rows)
    )
    segment_length = jnp.where(in_prompt, scalars[0], jnp.where(in_chosen, scalars[1], scalars[2]))
    valid = query_row - segment_start < segment_length
    query_limit = jnp.where(valid, query_row, -1)
    any_valid = first_row - segment_start < segment_length
    prompt_blocks = (prompt_length + BLOCK_K - 1) // BLOCK_K
    prompt_count = jnp.where(
        in_prompt, jnp.minimum(prompt_blocks, (first_row + span) // BLOCK_K), prompt_blocks
    )
    reply_count = jnp.where(
        in_prompt,
        0,
        jnp.minimum(
            (segment_length + BLOCK_K - 1) // BLOCK_K,
            (first_row + span - segment_start) // BLOCK_K,
        ),
    )
    prompt_count = jnp.where(any_valid, prompt_count, 0)
    total_count = jnp.where(any_valid, prompt_count + reply_count, 0)
    reply_base = segment_start // BLOCK_K - prompt_count

    def block_start(j):
        index = jnp.where(j < prompt_count, j, j + reply_base)
        return pl.multiple_of(index * BLOCK_K, BLOCK_K)

    key_iota = lax.broadcasted_iota(jnp.int32, (BLOCK_K, BLOCK_Q), 0)

    def forward(j, carry):
        numerator, total = carry
        start = block_start(j)
        slot = pl.multiple_of(j * BLOCK_K, BLOCK_K)
        key_end = jnp.where(j < prompt_count, prompt_length, segment_start + segment_length)
        threshold = jnp.minimum(query_limit, key_end - 1) - start
        raw = dot(keys[pl.ds(start, BLOCK_K), :], query, NT)
        cap = jnp.tanh(raw * (score_scale / soft_cap))
        weights = jnp.where(key_iota <= threshold, jnp.exp(cap * soft_cap), 0.0)
        cap_scr[pl.ds(slot, BLOCK_K), :] = cap
        weight_scr[pl.ds(slot, BLOCK_K), :] = weights
        numerator = numerator + dot(
            values_t[:, pl.ds(start, BLOCK_K)], weights.astype(jnp.bfloat16)
        )
        total = total + jnp.sum(weights, axis=0, keepdims=True)
        return numerator, total

    numerator, total = lax.fori_loop(
        0,
        total_count,
        forward,
        (
            jnp.zeros((HEAD_DIMENSION, BLOCK_Q), jnp.float32),
            jnp.zeros((1, BLOCK_Q), jnp.float32),
        ),
    )
    denominator = total + jnp.where(valid, 0.0, 1.0)
    inverse = 1.0 / denominator
    output = (numerator / denominator).astype(jnp.bfloat16).astype(jnp.float32)
    delta = jnp.sum(output * jnp.transpose(grad.astype(jnp.float32)), axis=0, keepdims=True)

    def backward(j, query_grad):
        start = block_start(j)
        slot = pl.multiple_of(j * BLOCK_K, BLOCK_K)
        cap = cap_scr[pl.ds(slot, BLOCK_K), :]
        prob = weight_scr[pl.ds(slot, BLOCK_K), :] * inverse
        grad_prob = dot(values[pl.ds(start, BLOCK_K), :], grad, NT)
        slope = (
            prob * (grad_prob - delta) * (score_scale - score_scale * cap * cap)
        ).astype(jnp.bfloat16)
        key_grad[pl.ds(start, BLOCK_K), :] += dot(slope, query)
        value_grad[pl.ds(start, BLOCK_K), :] += dot(prob.astype(jnp.bfloat16), grad)
        return query_grad + dot(keys_t[:, pl.ds(start, BLOCK_K)], slope)

    query_grad = lax.fori_loop(
        0, total_count, backward, jnp.zeros((HEAD_DIMENSION, BLOCK_Q), jnp.float32)
    )
    output_rows = jnp.transpose(output).astype(jnp.bfloat16)
    grad_rows = jnp.transpose(query_grad).astype(jnp.bfloat16)
    for s in range(count):
        back_ref[s, :sub_rows] = output_rows[s * sub_rows : (s + 1) * sub_rows]
        back_ref[s, sub_rows:] = grad_rows[s * sub_rows : (s + 1) * sub_rows]

    @pl.when(step == pl.num_programs(0) - 1)
    def _():
        keep_ref[...] = jnp.where(even, key_grad[...], value_grad[...])
        send_ref[...] = jnp.where(even, value_grad[...], key_grad[...])


def attention(scalars, received, own, other, parts, row_block):
    token_count = own.shape[0]
    sub_rows = row_block // parts
    count = BLOCK_Q // sub_rows
    steps = received.shape[0] // count
    whole = lambda: pl.BlockSpec((token_count, HEAD_DIMENSION), lambda i: (0, 0))
    pairs = token_count * token_count // parts
    return pl.pallas_call(
        functools.partial(attention_kernel, parts, row_block),
        grid=(steps,),
        in_specs=[
            pl.BlockSpec(memory_space=pltpu.SMEM),
            pl.BlockSpec((count, 2 * sub_rows, HEAD_DIMENSION), lambda i: (i, 0, 0)),
            whole(),
            whole(),
        ],
        out_specs=[
            pl.BlockSpec((count, 2 * sub_rows, HEAD_DIMENSION), lambda i: (i, 0, 0)),
            whole(),
            whole(),
        ],
        out_shape=[
            jax.ShapeDtypeStruct(received.shape, jnp.bfloat16),
            jax.ShapeDtypeStruct((token_count, HEAD_DIMENSION), jnp.float32),
            jax.ShapeDtypeStruct((token_count, HEAD_DIMENSION), jnp.float32),
        ],
        scratch_shapes=[
            pltpu.VMEM((token_count, HEAD_DIMENSION), jnp.bfloat16),
            pltpu.VMEM((token_count, HEAD_DIMENSION), jnp.bfloat16),
            pltpu.VMEM((HEAD_DIMENSION, token_count), jnp.bfloat16),
            pltpu.VMEM((HEAD_DIMENSION, token_count), jnp.bfloat16),
            pltpu.VMEM((token_count, HEAD_DIMENSION), jnp.float32),
            pltpu.VMEM((token_count, HEAD_DIMENSION), jnp.float32),
            pltpu.VMEM((token_count, BLOCK_Q), jnp.float32),
            pltpu.VMEM((token_count, BLOCK_Q), jnp.float32),
        ],
        compiler_params=pltpu.CompilerParams(vmem_limit_bytes=48 * 1024 * 1024),
        cost_estimate=pl.CostEstimate(
            flops=20 * pairs * HEAD_DIMENSION, bytes_accessed=8 * own.size, transcendentals=pairs
        ),
    )(scalars, received, own, other)


def input_grad_kernel(grad_ref, weight_ref, low_ref, down_ref, perm_ref, out_ref):
    perm = perm_ref[...]
    down = dot(down_ref[...].astype(jnp.bfloat16), perm).astype(jnp.bfloat16)
    mixed = dot(grad_ref[...], weight_ref[...], NT) + dot(low_ref[...], down)
    out_ref[...] = dot(mixed.astype(jnp.bfloat16), perm, NT).astype(jnp.bfloat16)


def input_grad(grad, weight, low, down, perm):
    rows = grad.shape[0]
    width, columns = weight.shape
    whole = lambda array: pl.BlockSpec(array.shape, lambda i: (0,) * array.ndim)
    return pl.pallas_call(
        input_grad_kernel,
        grid=(width // (4 * CHUNK),),
        in_specs=[
            whole(grad),
            pl.BlockSpec((4 * CHUNK, columns), lambda i: (i, 0)),
            whole(low),
            pl.BlockSpec((low.shape[1], 4 * CHUNK), lambda i: (0, i)),
            whole(perm),
        ],
        out_specs=pl.BlockSpec((rows, 4 * CHUNK), lambda i: (0, i)),
        out_shape=jax.ShapeDtypeStruct((rows, width), jnp.bfloat16),
        compiler_params=pltpu.CompilerParams(vmem_limit_bytes=40 * 1024 * 1024),
        cost_estimate=pl.CostEstimate(
            flops=2 * rows * width * columns, bytes_accessed=2 * width * columns, transcendentals=0
        ),
    )(grad, weight, low, down, perm)


def rope_tables(lengths, token_count):
    small = 64
    prompt_rows = 3 * token_count // 4
    reply_rows = token_count // 8
    start = jnp.arange(token_count // small, dtype=jnp.int32) * small
    position = jnp.where(
        start < prompt_rows, start, lengths[0] + lax.rem(start - prompt_rows, reply_rows)
    )
    half = HEAD_DIMENSION // 2
    inverse = rope_base ** (-2.0 * jnp.arange(half, dtype=jnp.float32) / HEAD_DIMENSION)
    large = position.astype(jnp.float32)[:, None] * inverse[None, :]
    little = jnp.arange(small, dtype=jnp.float32)[:, None] * inverse[None, :]
    double = lambda array: jnp.concatenate([array, array], axis=1)
    large_cos, large_sin = double(jnp.cos(large))[:, None], double(jnp.sin(large))[:, None]
    little_cos, little_sin = double(jnp.cos(little))[None], double(jnp.sin(little))[None]
    cosine = large_cos * little_cos - large_sin * little_sin
    sine = large_sin * little_cos + large_cos * little_sin
    sign = jnp.where(jnp.arange(HEAD_DIMENSION) < half, -1.0, 1.0).astype(jnp.float32)
    shape = (token_count, HEAD_DIMENSION)
    return cosine.reshape(shape), (sine * sign).reshape(shape)


def per_device(
    hidden,
    packed_weight_codes,
    block_scale_codes,
    grouped_scale,
    adapter_down_weight,
    key_up_weight,
    value_up_weight,
    queries,
    chosen_output_gradient,
    rejected_output_gradient,
    sequence_log_likelihoods,
    lengths,
):
    rows_here, width = hidden.shape
    seq_count = lax.axis_size("seq")
    me = lax.axis_index("seq")
    token_count = rows_here * seq_count
    prompt_rows = 3 * token_count // 4
    reply_rows = token_count // 8
    parts = seq_count // HEADS
    sub_rows = rows_here // parts
    parity = lax.rem(me, 2)
    part = lax.rem(me // 2, parts)

    own_rows = me * rows_here + jnp.arange(rows_here, dtype=jnp.int32)
    margin = dpo_beta * (
        sequence_log_likelihoods[0]
        - sequence_log_likelihoods[2]
        - (sequence_log_likelihoods[1] - sequence_log_likelihoods[3])
    )
    pair_weight = dpo_beta * jax.nn.sigmoid(-margin)
    in_chosen = (own_rows < prompt_rows + reply_rows).astype(jnp.float32)[:, None]
    in_rejected = ((own_rows < prompt_rows) | (own_rows >= prompt_rows + reply_rows)).astype(
        jnp.float32
    )[:, None]
    grad_out = (
        pair_weight
        * (
            rejected_output_gradient.astype(jnp.float32) * in_rejected
            - chosen_output_gradient.astype(jnp.float32) * in_chosen
        )
    ).astype(jnp.bfloat16)

    def exchange(array):
        return lax.all_to_all(array, "seq", split_axis=0, concat_axis=0, tiled=True)

    def swap(array):
        return lax.ppermute(array, "seq", [(i, i ^ 1) for i in range(seq_count)])

    def to_heads(array):
        split = array.reshape(parts, sub_rows, KEY_VALUE_HEADS, 2, HEAD_DIMENSION)
        return jnp.transpose(split, (2, 0, 3, 1, 4)).reshape(seq_count, sub_rows, HEAD_DIMENSION)

    received = exchange(jnp.concatenate([to_heads(queries), to_heads(grad_out)], axis=1))

    cosine, sine = rope_tables(lengths, token_count)
    own_cosine = lax.dynamic_slice_in_dim(cosine, me * rows_here, rows_here, 0)
    own_sine = lax.dynamic_slice_in_dim(sine, me * rows_here, rows_here, 0)
    columns = packed_weight_codes.shape[1]
    group_count = grouped_scale.shape[1]
    spread = jnp.repeat(grouped_scale, columns // group_count, axis=1)
    absmax = spread * (block_scale_codes.astype(jnp.float32) + 1.0) / 256.0
    table = jnp.zeros((CHUNK, 128), jnp.float32) + jnp.pad(
        jnp.array(nf4_levels, jnp.float32), (0, 112)
    )
    source = jnp.arange(4 * CHUNK)
    perm = (source[:, None] == (4 * (source % CHUNK) + source // CHUNK)[None, :]).astype(
        jnp.bfloat16
    )
    weight, hidden_t, kv, low_rank = project(
        hidden,
        packed_weight_codes,
        absmax,
        table,
        perm,
        adapter_down_weight,
        key_up_weight,
        value_up_weight,
        own_cosine,
        own_sine,
    )
    if parts > 1:
        kv = jnp.broadcast_to(
            kv.reshape(KEY_VALUE_HEADS, 1, 2, rows_here, HEAD_DIMENSION),
            (KEY_VALUE_HEADS, parts, 2, rows_here, HEAD_DIMENSION),
        ).reshape(seq_count, rows_here, HEAD_DIMENSION)
    own = exchange(kv).reshape(token_count, HEAD_DIMENSION)
    other = swap(own)
    hidden_t, low_rank_later, other = lax.optimization_barrier((hidden_t, low_rank, other))
    hidden_columns = exchange(hidden_t.reshape(seq_count, width // seq_count, rows_here))
    low_all = lax.all_gather(low_rank_later, "seq", axis=0, tiled=True)

    scalars = jnp.concatenate([lengths, jnp.stack([parity, part]).astype(jnp.int32)])
    back, keep, send = attention(scalars, received, own, other, parts, rows_here)
    total = keep + swap(send)
    if parts > 1:
        groups = [
            [2 * parts * h + 2 * r + c for r in range(parts)]
            for h in range(KEY_VALUE_HEADS)
            for c in range(2)
        ]
        total = lax.psum(total, "seq", axis_index_groups=groups)
    half = HEAD_DIMENSION // 2
    turned = total * cosine - jnp.roll(total, half, axis=1) * sine
    grad_column = jnp.where(parity == 0, turned, total).astype(jnp.bfloat16)
    low_here = jnp.where(parity == 0, low_all[:, :ADAPTER_RANK], low_all[:, ADAPTER_RANK:])
    up_grad = adapter_multiplier * lax.dot_general(
        low_here, grad_column, (((0,), (0,)), ((), ())), preferred_element_type=jnp.float32
    )
    gathered = exchange(grad_column.reshape(seq_count, rows_here, HEAD_DIMENSION))
    pieces = gathered.reshape(KEY_VALUE_HEADS, parts, 2, rows_here, HEAD_DIMENSION)[:, 0]
    projection_gradient = jnp.transpose(pieces, (2, 1, 0, 3)).reshape(rows_here, -1)
    key_width = KEY_VALUE_HEADS * HEAD_DIMENSION
    low_gradient = (
        adapter_multiplier
        * jnp.concatenate(
            [
                dot(projection_gradient[:, :key_width], key_up_weight.astype(jnp.bfloat16), NT),
                dot(projection_gradient[:, key_width:], value_up_weight.astype(jnp.bfloat16), NT),
            ],
            axis=1,
        )
    ).astype(jnp.bfloat16)
    low_gradient_all = lax.all_gather(low_gradient, "seq", axis=0, tiled=False)
    back, low_gradient = lax.optimization_barrier((back, low_gradient))
    returned = exchange(back)
    hidden_gradient = input_grad(
        projection_gradient, weight, low_gradient, adapter_down_weight, perm
    )
    down_slice = lax.dot_general(
        jnp.transpose(hidden_columns, (1, 0, 2)).reshape(width // seq_count, token_count),
        low_gradient_all.reshape(token_count, 2 * ADAPTER_RANK),
        NN,
        preferred_element_type=jnp.float32,
    )
    finals = lax.all_gather(
        jnp.concatenate([down_slice, up_grad], axis=0).astype(jnp.bfloat16), "seq", axis=0
    )
    slice_rows = width // seq_count
    adapter_down_gradient = jnp.transpose(
        finals[:, :slice_rows].reshape(width, 2 * ADAPTER_RANK)
    ).astype(jnp.float32)
    ups = finals[:, slice_rows:].reshape(
        KEY_VALUE_HEADS, parts, 2, ADAPTER_RANK, HEAD_DIMENSION
    )[:, 0]
    ups = jnp.transpose(ups, (1, 2, 0, 3)).reshape(2, ADAPTER_RANK, key_width).astype(jnp.float32)

    def from_heads(array):
        split = array.reshape(KEY_VALUE_HEADS, parts, 2, sub_rows, HEAD_DIMENSION)
        return jnp.transpose(split, (1, 3, 0, 2, 4)).reshape(rows_here, HEADS * HEAD_DIMENSION)

    return (
        from_heads(returned[:, :sub_rows]),
        from_heads(returned[:, sub_rows:]),
        hidden_gradient,
        adapter_down_gradient,
        ups[0],
        ups[1],
    )


def solution(mesh):
    rows = P(("groups", "seq"), None)
    in_specs = (rows,) + (P(),) * 6 + (rows,) * 3 + (P("groups"),) * 2
    out_specs = (rows,) * 3 + (P("groups", None),) * 3
    return jax.shard_map(
        per_device, mesh=mesh, in_specs=in_specs, out_specs=out_specs, check_vma=False
    )
```

```python
import functools

import jax
import jax.numpy as jnp
from jax import lax
from jax.experimental import pallas as pl
from jax.experimental.pallas import tpu as pltpu
from jax.sharding import PartitionSpec as P

HEADS = 16
KEY_VALUE_HEADS = 8
HEAD_DIMENSION = 128
ADAPTER_RANK = 64
CHUNK = 128
BLOCK_Q = 256
BLOCK_K = 256

nf4_levels = (
    -1.0,
    -0.6961928009986877,
    -0.5250730514526367,
    -0.39491748809814453,
    -0.28444138169288635,
    -0.18477343022823334,
    -0.09105003625154495,
    0.0,
    0.07958029955625534,
    0.16093020141124725,
    0.24611230194568634,
    0.33791524171829224,
    0.44070982933044434,
    0.5626170039176941,
    0.7229568362236023,
    1.0,
)
score_scale = 1.0 / 12.0
soft_cap = 50.0
dpo_beta = 0.5
adapter_multiplier = 0.5
rope_base = 10000.0

NT = (((1,), (1,)), ((), ()))
NN = (((1,), (0,)), ((), ()))


def dot(a, b, dims=NN):
    return lax.dot_general(a, b, dims, preferred_element_type=jnp.float32)


def project_kernel(
    hidden_ref,
    codes_ref,
    absmax_ref,
    table_ref,
    perm_ref,
    down_ref,
    key_up_ref,
    value_up_ref,
    cos_ref,
    sin_ref,
    weight_ref,
    hidden_t_ref,
    kv_ref,
    low_ref,
    acc,
    low_acc,
):
    step = pl.program_id(0)

    @pl.when(step == 0)
    def _():
        acc[...] = jnp.zeros_like(acc)
        low_acc[...] = jnp.zeros_like(low_acc)

    hidden = hidden_ref[...]
    hidden_t_ref[...] = jnp.transpose(hidden.astype(jnp.float32)).astype(jnp.bfloat16)
    permuted = dot(hidden, perm_ref[...]).astype(jnp.bfloat16)
    low_acc[...] += dot(hidden, down_ref[...].astype(jnp.bfloat16), NT)
    rows, columns = codes_ref.shape
    blocks = absmax_ref.shape[0]
    table = table_ref[...]
    for column in range(0, columns, 128):
        span = slice(column, column + 128)
        scale = jnp.broadcast_to(
            absmax_ref[:, span][:, None, :], (blocks, rows // blocks, 128)
        ).reshape(rows, 128)
        codes = codes_ref[:, span]
        for nibble in range(4):
            index = lax.bitwise_and(lax.shift_right_logical(codes, 4 * nibble), 15)
            level = jnp.take_along_axis(table, index, axis=1, mode="promise_in_bounds")
            weight_ref[nibble * rows : (nibble + 1) * rows, span] = (level * scale).astype(
                jnp.bfloat16
            )
    acc[...] += dot(permuted, weight_ref[...])

    @pl.when(step == pl.num_programs(0) - 1)
    def _():
        low = low_acc[...].astype(jnp.bfloat16)
        low_ref[...] = low
        key_add = adapter_multiplier * dot(
            low[:, :ADAPTER_RANK], key_up_ref[...].astype(jnp.bfloat16)
        )
        value_add = adapter_multiplier * dot(
            low[:, ADAPTER_RANK:], value_up_ref[...].astype(jnp.bfloat16)
        )
        cosine = cos_ref[...]
        sine = sin_ref[...]
        width = KEY_VALUE_HEADS * HEAD_DIMENSION
        for head in range(KEY_VALUE_HEADS):
            span = slice(head * HEAD_DIMENSION, (head + 1) * HEAD_DIMENSION)
            linear = acc[:, span] + key_add[:, span]
            turned = linear * cosine + pltpu.roll(linear, HEAD_DIMENSION // 2, 1) * sine
            kv_ref[2 * head] = turned.astype(jnp.bfloat16)
            kv_ref[2 * head + 1] = (
                acc[:, width + head * HEAD_DIMENSION : width + (head + 1) * HEAD_DIMENSION]
                + value_add[:, span]
            ).astype(jnp.bfloat16)


def project(hidden, codes, absmax, table, perm, down, key_up, value_up, cosine, sine):
    rows, width = hidden.shape
    columns = codes.shape[1]
    steps = codes.shape[0] // CHUNK
    blocks = absmax.shape[0] // steps
    whole = lambda array: pl.BlockSpec(array.shape, lambda i: (0,) * array.ndim)
    return pl.pallas_call(
        project_kernel,
        grid=(steps,),
        in_specs=[
            pl.BlockSpec((rows, 4 * CHUNK), lambda i: (0, i)),
            pl.BlockSpec((CHUNK, columns), lambda i: (i, 0)),
            pl.BlockSpec((blocks, columns), lambda i: (i, 0)),
            whole(table),
            whole(perm),
            pl.BlockSpec((2 * ADAPTER_RANK, 4 * CHUNK), lambda i: (0, i)),
            whole(key_up),
            whole(value_up),
            whole(cosine),
            whole(sine),
        ],
        out_specs=[
            pl.BlockSpec((4 * CHUNK, columns), lambda i: (i, 0)),
            pl.BlockSpec((4 * CHUNK, rows), lambda i: (i, 0)),
            pl.BlockSpec((2 * KEY_VALUE_HEADS, rows, HEAD_DIMENSION), lambda i: (0, 0, 0)),
            pl.BlockSpec((rows, 2 * ADAPTER_RANK), lambda i: (0, 0)),
        ],
        out_shape=[
            jax.ShapeDtypeStruct((width, columns), jnp.bfloat16),
            jax.ShapeDtypeStruct((width, rows), jnp.bfloat16),
            jax.ShapeDtypeStruct((2 * KEY_VALUE_HEADS, rows, HEAD_DIMENSION), jnp.bfloat16),
            jax.ShapeDtypeStruct((rows, 2 * ADAPTER_RANK), jnp.bfloat16),
        ],
        scratch_shapes=[
            pltpu.VMEM((rows, columns), jnp.float32),
            pltpu.VMEM((rows, 2 * ADAPTER_RANK), jnp.float32),
        ],
        compiler_params=pltpu.CompilerParams(vmem_limit_bytes=40 * 1024 * 1024),
        cost_estimate=pl.CostEstimate(
            flops=16 * rows * width * columns,
            bytes_accessed=4 * codes.size + 2 * width * columns,
            transcendentals=0,
        ),
    )(hidden, codes, absmax, table, perm, down, key_up, value_up, cosine, sine)


def attention_kernel(
    parts,
    row_block,
    scalars,
    qg_ref,
    own_ref,
    other_ref,
    back_ref,
    keep_ref,
    send_ref,
    keys,
    values,
    keys_t,
    values_t,
    key_grad,
    value_grad,
    cap_scr,
    weight_scr,
):
    step = pl.program_id(0)
    token_count = keys.shape[0]
    prompt_rows = 3 * token_count // 4
    reply_rows = token_count // 8
    sub_rows = row_block // parts
    even = scalars[3] == 0
    prompt_length = scalars[0]

    @pl.when(step == 0)
    def _():
        own = own_ref[...]
        other = other_ref[...]
        key = jnp.where(even, own.astype(jnp.float32), other.astype(jnp.float32))
        value = jnp.where(even, other.astype(jnp.float32), own.astype(jnp.float32))
        keys[...] = key.astype(jnp.bfloat16)
        values[...] = value.astype(jnp.bfloat16)
        keys_t[...] = jnp.transpose(key).astype(jnp.bfloat16)
        values_t[...] = jnp.transpose(value).astype(jnp.bfloat16)
        key_grad[...] = jnp.zeros_like(key_grad)
        value_grad[...] = jnp.zeros_like(value_grad)

    count = BLOCK_Q // sub_rows
    query = jnp.concatenate([qg_ref[s, :sub_rows] for s in range(count)], axis=0)
    grad = jnp.concatenate([qg_ref[s, sub_rows:] for s in range(count)], axis=0)

    lane = lax.broadcasted_iota(jnp.int32, (1, BLOCK_Q), 1)
    span = BLOCK_Q * parts
    first_row = step * span
    query_row = first_row + (lane // sub_rows) * row_block + scalars[4] * sub_rows + lane % sub_rows
    in_prompt = first_row < prompt_rows
    in_chosen = first_row < prompt_rows + reply_rows
    segment_start = jnp.where(
        in_prompt, 0, jnp.where(in_chosen, prompt_rows, prompt_rows + reply_rows)
    )
    segment_length = jnp.where(in_prompt, scalars[0], jnp.where(in_chosen, scalars[1], scalars[2]))
    valid = query_row - segment_start < segment_length
    query_limit = jnp.where(valid, query_row, -1)
    any_valid = first_row - segment_start < segment_length
    prompt_blocks = (prompt_length + BLOCK_K - 1) // BLOCK_K
    prompt_count = jnp.where(
        in_prompt, jnp.minimum(prompt_blocks, (first_row + span) // BLOCK_K), prompt_blocks
    )
    reply_count = jnp.where(
        in_prompt,
        0,
        jnp.minimum(
            (segment_length + BLOCK_K - 1) // BLOCK_K,
            (first_row + span - segment_start) // BLOCK_K,
        ),
    )
    prompt_count = jnp.where(any_valid, prompt_count, 0)
    total_count = jnp.where(any_valid, prompt_count + reply_count, 0)
    reply_base = segment_start // BLOCK_K - prompt_count

    def block_start(j):
        index = jnp.where(j < prompt_count, j, j + reply_base)
        return pl.multiple_of(index * BLOCK_K, BLOCK_K)

    key_iota = lax.broadcasted_iota(jnp.int32, (BLOCK_K, BLOCK_Q), 0)

    def forward(j, carry):
        numerator, total = carry
        start = block_start(j)
        slot = pl.multiple_of(j * BLOCK_K, BLOCK_K)
        key_end = jnp.where(j < prompt_count, prompt_length, segment_start + segment_length)
        threshold = jnp.minimum(query_limit, key_end - 1) - start
        raw = dot(keys[pl.ds(start, BLOCK_K), :], query, NT)
        cap = jnp.tanh(raw * (score_scale / soft_cap))
        weights = jnp.where(key_iota <= threshold, jnp.exp(cap * soft_cap), 0.0)
        cap_scr[pl.ds(slot, BLOCK_K), :] = cap
        weight_scr[pl.ds(slot, BLOCK_K), :] = weights
        numerator = numerator + dot(
            values_t[:, pl.ds(start, BLOCK_K)], weights.astype(jnp.bfloat16)
        )
        total = total + jnp.sum(weights, axis=0, keepdims=True)
        return numerator, total

    numerator, total = lax.fori_loop(
        0,
        total_count,
        forward,
        (
            jnp.zeros((HEAD_DIMENSION, BLOCK_Q), jnp.float32),
            jnp.zeros((1, BLOCK_Q), jnp.float32),
        ),
    )
    denominator = total + jnp.where(valid, 0.0, 1.0)
    inverse = 1.0 / denominator
    output = (numerator / denominator).astype(jnp.bfloat16).astype(jnp.float32)
    delta = jnp.sum(output * jnp.transpose(grad.astype(jnp.float32)), axis=0, keepdims=True)

    def backward(j, query_grad):
        start = block_start(j)
        slot = pl.multiple_of(j * BLOCK_K, BLOCK_K)
        cap = cap_scr[pl.ds(slot, BLOCK_K), :]
        prob = weight_scr[pl.ds(slot, BLOCK_K), :] * inverse
        grad_prob = dot(values[pl.ds(start, BLOCK_K), :], grad, NT)
        slope = (
            prob * (grad_prob - delta) * (score_scale - score_scale * cap * cap)
        ).astype(jnp.bfloat16)
        key_grad[pl.ds(start, BLOCK_K), :] += dot(slope, query)
        value_grad[pl.ds(start, BLOCK_K), :] += dot(prob.astype(jnp.bfloat16), grad)
        return query_grad + dot(keys_t[:, pl.ds(start, BLOCK_K)], slope)

    query_grad = lax.fori_loop(
        0, total_count, backward, jnp.zeros((HEAD_DIMENSION, BLOCK_Q), jnp.float32)
    )
    output_rows = jnp.transpose(output).astype(jnp.bfloat16)
    grad_rows = jnp.transpose(query_grad).astype(jnp.bfloat16)
    for s in range(count):
        back_ref[s, :sub_rows] = output_rows[s * sub_rows : (s + 1) * sub_rows]
        back_ref[s, sub_rows:] = grad_rows[s * sub_rows : (s + 1) * sub_rows]

    @pl.when(step == pl.num_programs(0) - 1)
    def _():
        keep_ref[...] = jnp.where(even, key_grad[...], value_grad[...])
        send_ref[...] = jnp.where(even, value_grad[...], key_grad[...])


def attention(scalars, received, own, other, parts, row_block):
    token_count = own.shape[0]
    sub_rows = row_block // parts
    count = BLOCK_Q // sub_rows
    steps = received.shape[0] // count
    whole = lambda: pl.BlockSpec((token_count, HEAD_DIMENSION), lambda i: (0, 0))
    pairs = token_count * token_count // parts
    return pl.pallas_call(
        functools.partial(attention_kernel, parts, row_block),
        grid=(steps,),
        in_specs=[
            pl.BlockSpec(memory_space=pltpu.SMEM),
            pl.BlockSpec((count, 2 * sub_rows, HEAD_DIMENSION), lambda i: (i, 0, 0)),
            whole(),
            whole(),
        ],
        out_specs=[
            pl.BlockSpec((count, 2 * sub_rows, HEAD_DIMENSION), lambda i: (i, 0, 0)),
            whole(),
            whole(),
        ],
        out_shape=[
            jax.ShapeDtypeStruct(received.shape, jnp.bfloat16),
            jax.ShapeDtypeStruct((token_count, HEAD_DIMENSION), jnp.float32),
            jax.ShapeDtypeStruct((token_count, HEAD_DIMENSION), jnp.float32),
        ],
        scratch_shapes=[
            pltpu.VMEM((token_count, HEAD_DIMENSION), jnp.bfloat16),
            pltpu.VMEM((token_count, HEAD_DIMENSION), jnp.bfloat16),
            pltpu.VMEM((HEAD_DIMENSION, token_count), jnp.bfloat16),
            pltpu.VMEM((HEAD_DIMENSION, token_count), jnp.bfloat16),
            pltpu.VMEM((token_count, HEAD_DIMENSION), jnp.float32),
            pltpu.VMEM((token_count, HEAD_DIMENSION), jnp.float32),
            pltpu.VMEM((token_count, BLOCK_Q), jnp.float32),
            pltpu.VMEM((token_count, BLOCK_Q), jnp.float32),
        ],
        compiler_params=pltpu.CompilerParams(vmem_limit_bytes=48 * 1024 * 1024),
        cost_estimate=pl.CostEstimate(
            flops=60 * pairs * HEAD_DIMENSION, bytes_accessed=8 * own.size, transcendentals=pairs
        ),
    )(scalars, received, own, other)


def input_grad_kernel(grad_ref, weight_ref, low_ref, down_ref, perm_ref, out_ref):
    perm = perm_ref[...]
    down = dot(down_ref[...].astype(jnp.bfloat16), perm).astype(jnp.bfloat16)
    mixed = dot(grad_ref[...], weight_ref[...], NT) + dot(low_ref[...], down)
    out_ref[...] = dot(mixed.astype(jnp.bfloat16), perm, NT).astype(jnp.bfloat16)


def input_grad(grad, weight, low, down, perm):
    rows = grad.shape[0]
    width, columns = weight.shape
    whole = lambda array: pl.BlockSpec(array.shape, lambda i: (0,) * array.ndim)
    return pl.pallas_call(
        input_grad_kernel,
        grid=(width // (4 * CHUNK),),
        in_specs=[
            whole(grad),
            pl.BlockSpec((4 * CHUNK, columns), lambda i: (i, 0)),
            whole(low),
            pl.BlockSpec((low.shape[1], 4 * CHUNK), lambda i: (0, i)),
            whole(perm),
        ],
        out_specs=pl.BlockSpec((rows, 4 * CHUNK), lambda i: (0, i)),
        out_shape=jax.ShapeDtypeStruct((rows, width), jnp.bfloat16),
        compiler_params=pltpu.CompilerParams(vmem_limit_bytes=40 * 1024 * 1024),
        cost_estimate=pl.CostEstimate(
            flops=8 * rows * width * columns, bytes_accessed=2 * width * columns, transcendentals=0
        ),
    )(grad, weight, low, down, perm)


def gather_heads_kernel(parts, scalars, query_ref, chosen_ref, rejected_ref, out_ref):
    rows = query_ref.shape[0]
    sub_rows = rows // parts
    for part in range(parts):
        span = slice(part * sub_rows, (part + 1) * sub_rows)
        for head in range(HEADS):
            place = (head // 2 * parts + part) * 2 + head % 2
            lanes = slice(head * HEAD_DIMENSION, (head + 1) * HEAD_DIMENSION)
            out_ref[place, :sub_rows] = query_ref[span, lanes]
            out_ref[place, sub_rows:] = (
                scalars[0]
                * (
                    rejected_ref[span, lanes].astype(jnp.float32) * scalars[2]
                    - chosen_ref[span, lanes].astype(jnp.float32) * scalars[1]
                )
            ).astype(jnp.bfloat16)


def gather_heads(scalars, queries, chosen, rejected, parts):
    rows, width = queries.shape
    return pl.pallas_call(
        functools.partial(gather_heads_kernel, parts),
        in_specs=[pl.BlockSpec(memory_space=pltpu.SMEM)]
        + [pl.BlockSpec(memory_space=pltpu.VMEM)] * 3,
        out_specs=pl.BlockSpec(memory_space=pltpu.VMEM),
        out_shape=jax.ShapeDtypeStruct(
            (HEADS * parts, 2 * rows // parts, HEAD_DIMENSION), jnp.bfloat16
        ),
        compiler_params=pltpu.CompilerParams(vmem_limit_bytes=16 * 1024 * 1024),
    )(scalars, queries, chosen, rejected)


def scatter_heads_kernel(parts, back_ref, output_ref, grad_ref):
    sub_rows = output_ref.shape[0] // parts
    for part in range(parts):
        span = slice(part * sub_rows, (part + 1) * sub_rows)
        for head in range(HEADS):
            place = (head // 2 * parts + part) * 2 + head % 2
            lanes = slice(head * HEAD_DIMENSION, (head + 1) * HEAD_DIMENSION)
            output_ref[span, lanes] = back_ref[place, :sub_rows]
            grad_ref[span, lanes] = back_ref[place, sub_rows:]


def scatter_heads(back, parts):
    shape = jax.ShapeDtypeStruct(
        (back.shape[1] // 2 * parts, HEADS * HEAD_DIMENSION), jnp.bfloat16
    )
    return pl.pallas_call(
        functools.partial(scatter_heads_kernel, parts),
        in_specs=[pl.BlockSpec(memory_space=pltpu.VMEM)],
        out_specs=[pl.BlockSpec(memory_space=pltpu.VMEM)] * 2,
        out_shape=[shape, shape],
        compiler_params=pltpu.CompilerParams(vmem_limit_bytes=16 * 1024 * 1024),
    )(back)


def rope_tables(lengths, token_count):
    small = 64
    prompt_rows = 3 * token_count // 4
    reply_rows = token_count // 8
    start = jnp.arange(token_count // small, dtype=jnp.int32) * small
    position = jnp.where(
        start < prompt_rows, start, lengths[0] + lax.rem(start - prompt_rows, reply_rows)
    )
    half = HEAD_DIMENSION // 2
    inverse = rope_base ** (-2.0 * jnp.arange(half, dtype=jnp.float32) / HEAD_DIMENSION)
    large = position.astype(jnp.float32)[:, None] * inverse[None, :]
    little = jnp.arange(small, dtype=jnp.float32)[:, None] * inverse[None, :]
    double = lambda array: jnp.concatenate([array, array], axis=1)
    large_cos, large_sin = double(jnp.cos(large))[:, None], double(jnp.sin(large))[:, None]
    little_cos, little_sin = double(jnp.cos(little))[None], double(jnp.sin(little))[None]
    cosine = large_cos * little_cos - large_sin * little_sin
    sine = large_sin * little_cos + large_cos * little_sin
    sign = jnp.where(jnp.arange(HEAD_DIMENSION) < half, -1.0, 1.0).astype(jnp.float32)
    shape = (token_count, HEAD_DIMENSION)
    return cosine.reshape(shape), (sine * sign).reshape(shape)


def per_device(
    hidden,
    packed_weight_codes,
    block_scale_codes,
    grouped_scale,
    adapter_down_weight,
    key_up_weight,
    value_up_weight,
    queries,
    chosen_output_gradient,
    rejected_output_gradient,
    sequence_log_likelihoods,
    lengths,
):
    rows_here, width = hidden.shape
    seq_count = lax.axis_size("seq")
    me = lax.axis_index("seq")
    token_count = rows_here * seq_count
    prompt_rows = 3 * token_count // 4
    reply_rows = token_count // 8
    parts = seq_count // HEADS
    parity = lax.rem(me, 2)
    part = lax.rem(me // 2, parts)

    margin = dpo_beta * (
        sequence_log_likelihoods[0]
        - sequence_log_likelihoods[2]
        - (sequence_log_likelihoods[1] - sequence_log_likelihoods[3])
    )
    pair_weight = dpo_beta * jax.nn.sigmoid(-margin)
    first_row = me * rows_here
    in_chosen = jnp.where(first_row < prompt_rows + reply_rows, 1.0, 0.0)
    in_rejected = jnp.where(
        (first_row < prompt_rows) | (first_row >= prompt_rows + reply_rows), 1.0, 0.0
    )

    def exchange(array):
        return lax.all_to_all(array, "seq", split_axis=0, concat_axis=0, tiled=True)

    def swap(array):
        return lax.ppermute(array, "seq", [(i, i ^ 1) for i in range(seq_count)])

    sent = gather_heads(
        jnp.stack([pair_weight, in_chosen, in_rejected]),
        queries,
        chosen_output_gradient,
        rejected_output_gradient,
        parts,
    )
    sent, codes = lax.optimization_barrier((sent, packed_weight_codes))
    received = exchange(sent)

    cosine, sine = rope_tables(lengths, token_count)
    own_cosine = lax.dynamic_slice_in_dim(cosine, me * rows_here, rows_here, 0)
    own_sine = lax.dynamic_slice_in_dim(sine, me * rows_here, rows_here, 0)
    columns = packed_weight_codes.shape[1]
    group_count = grouped_scale.shape[1]
    spread = jnp.repeat(grouped_scale, columns // group_count, axis=1)
    absmax = spread * (block_scale_codes.astype(jnp.float32) + 1.0) / 256.0
    table = jnp.zeros((CHUNK, 128), jnp.float32) + jnp.pad(
        jnp.array(nf4_levels, jnp.float32), (0, 112)
    )
    source = jnp.arange(4 * CHUNK)
    perm = (source[:, None] == (4 * (source % CHUNK) + source // CHUNK)[None, :]).astype(
        jnp.bfloat16
    )
    weight, hidden_t, kv, low_rank = project(
        hidden,
        codes,
        absmax,
        table,
        perm,
        adapter_down_weight,
        key_up_weight,
        value_up_weight,
        own_cosine,
        own_sine,
    )
    if parts > 1:
        kv = jnp.broadcast_to(
            kv.reshape(KEY_VALUE_HEADS, 1, 2, rows_here, HEAD_DIMENSION),
            (KEY_VALUE_HEADS, parts, 2, rows_here, HEAD_DIMENSION),
        ).reshape(seq_count, rows_here, HEAD_DIMENSION)
    kv, received = lax.optimization_barrier((kv, received))
    own = exchange(kv).reshape(token_count, HEAD_DIMENSION)
    other = swap(own)
    low_halves = jnp.transpose(low_rank).reshape(1, 2, ADAPTER_RANK, rows_here)
    early = jnp.concatenate(
        [
            hidden_t.reshape(seq_count, width // seq_count, rows_here),
            jnp.broadcast_to(
                low_halves, (seq_count // 2, 2, ADAPTER_RANK, rows_here)
            ).reshape(seq_count, ADAPTER_RANK, rows_here),
        ],
        axis=1,
    )
    early, other = lax.optimization_barrier((early, other))
    early = exchange(early)

    scalars = jnp.concatenate([lengths, jnp.stack([parity, part]).astype(jnp.int32)])
    back, keep, send = attention(scalars, received, own, other, parts, rows_here)
    send, early = lax.optimization_barrier((send, early))
    total = keep + swap(send)
    if parts > 1:
        groups = [
            [2 * parts * h + 2 * r + c for r in range(parts)]
            for h in range(KEY_VALUE_HEADS)
            for c in range(2)
        ]
        total = lax.psum(total, "seq", axis_index_groups=groups)
    half = HEAD_DIMENSION // 2
    turned = total * cosine - jnp.roll(total, half, axis=1) * sine
    grad_column = jnp.where(parity == 0, turned, total).astype(jnp.bfloat16)
    slice_rows = width // seq_count
    early = jnp.transpose(early, (1, 0, 2)).reshape(slice_rows + ADAPTER_RANK, token_count)
    up_grad = adapter_multiplier * dot(early[slice_rows:], grad_column)
    gathered = exchange(grad_column.reshape(seq_count, rows_here, HEAD_DIMENSION))
    pieces = gathered.reshape(KEY_VALUE_HEADS, parts, 2, rows_here, HEAD_DIMENSION)[:, 0]
    projection_gradient = jnp.transpose(pieces, (2, 1, 0, 3)).reshape(rows_here, -1)
    key_width = KEY_VALUE_HEADS * HEAD_DIMENSION
    low_gradient = (
        adapter_multiplier
        * jnp.concatenate(
            [
                dot(projection_gradient[:, :key_width], key_up_weight.astype(jnp.bfloat16), NT),
                dot(projection_gradient[:, key_width:], value_up_weight.astype(jnp.bfloat16), NT),
            ],
            axis=1,
        )
    ).astype(jnp.bfloat16)
    low_gradient_all = exchange(
        jnp.broadcast_to(low_gradient[None], (seq_count, rows_here, 2 * ADAPTER_RANK))
    )
    hidden_gradient = input_grad(
        projection_gradient, weight, low_gradient, adapter_down_weight, perm
    )
    low_gradient_all, hidden_gradient, back = lax.optimization_barrier(
        (low_gradient_all, hidden_gradient, back)
    )
    down_slice = dot(
        early[:slice_rows], low_gradient_all.reshape(token_count, 2 * ADAPTER_RANK)
    )
    finals = lax.all_gather(
        jnp.concatenate([down_slice, up_grad], axis=0).astype(jnp.bfloat16), "seq", axis=0
    )
    returned = exchange(back)
    adapter_down_gradient = jnp.transpose(
        finals[:, :slice_rows].reshape(width, 2 * ADAPTER_RANK)
    ).astype(jnp.float32)
    ups = finals[:, slice_rows:].reshape(
        KEY_VALUE_HEADS, parts, 2, ADAPTER_RANK, HEAD_DIMENSION
    )[:, 0]
    ups = jnp.transpose(ups, (1, 2, 0, 3)).reshape(2, ADAPTER_RANK, key_width).astype(jnp.float32)

    attention_output, query_gradient = scatter_heads(returned, parts)
    return (
        attention_output,
        query_gradient,
        hidden_gradient,
        adapter_down_gradient,
        ups[0],
        ups[1],
    )


def solution(mesh):
    rows = P(("groups", "seq"), None)
    in_specs = (rows,) + (P(),) * 6 + (rows,) * 3 + (P("groups"),) * 2
    out_specs = (rows,) * 3 + (P("groups", None),) * 3
    return jax.shard_map(
        per_device, mesh=mesh, in_specs=in_specs, out_specs=out_specs, check_vma=False
    )
```

```python
import functools

import jax
import jax.numpy as jnp
from jax import lax
from jax.experimental import pallas as pl
from jax.experimental.pallas import tpu as pltpu
from jax.sharding import PartitionSpec as P

HEADS = 16
KEY_VALUE_HEADS = 8
HEAD_DIMENSION = 128
ADAPTER_RANK = 64
CHUNK = 128
BLOCK_Q = 256
BLOCK_K = 256

nf4_levels = (
    -1.0,
    -0.6961928009986877,
    -0.5250730514526367,
    -0.39491748809814453,
    -0.28444138169288635,
    -0.18477343022823334,
    -0.09105003625154495,
    0.0,
    0.07958029955625534,
    0.16093020141124725,
    0.24611230194568634,
    0.33791524171829224,
    0.44070982933044434,
    0.5626170039176941,
    0.7229568362236023,
    1.0,
)
score_scale = 1.0 / 12.0
soft_cap = 50.0
dpo_beta = 0.5
adapter_multiplier = 0.5
rope_base = 10000.0

NT = (((1,), (1,)), ((), ()))
NN = (((1,), (0,)), ((), ()))


def dot(a, b, dims=NN):
    return lax.dot_general(a, b, dims, preferred_element_type=jnp.float32)


def project_kernel(
    hidden_ref,
    codes_ref,
    absmax_ref,
    table_ref,
    perm_ref,
    down_ref,
    key_up_ref,
    value_up_ref,
    cos_ref,
    sin_ref,
    weight_ref,
    hidden_t_ref,
    kv_ref,
    low_ref,
    acc,
    low_acc,
):
    step = pl.program_id(0)

    @pl.when(step == 0)
    def _():
        acc[...] = jnp.zeros_like(acc)
        low_acc[...] = jnp.zeros_like(low_acc)

    hidden = hidden_ref[...]
    hidden_t_ref[...] = jnp.transpose(hidden.astype(jnp.float32)).astype(jnp.bfloat16)
    permuted = dot(hidden, perm_ref[...]).astype(jnp.bfloat16)
    low_acc[...] += dot(hidden, down_ref[...].astype(jnp.bfloat16), NT)
    rows, columns = codes_ref.shape
    blocks = absmax_ref.shape[0]
    table = table_ref[...]
    for column in range(0, columns, 128):
        span = slice(column, column + 128)
        scale = jnp.broadcast_to(
            absmax_ref[:, span][:, None, :], (blocks, rows // blocks, 128)
        ).reshape(rows, 128)
        codes = codes_ref[:, span]
        for nibble in range(4):
            index = lax.bitwise_and(lax.shift_right_logical(codes, 4 * nibble), 15)
            level = jnp.take_along_axis(table, index, axis=1, mode="promise_in_bounds")
            weight_ref[nibble * rows : (nibble + 1) * rows, span] = (level * scale).astype(
                jnp.bfloat16
            )
        if column % 256 == 128:
            pair = slice(column - 128, column + 128)
            acc[:, pair] += dot(permuted, weight_ref[:, pair])

    @pl.when(step == pl.num_programs(0) - 1)
    def _():
        low = low_acc[...].astype(jnp.bfloat16)
        low_ref[...] = low
        key_add = adapter_multiplier * dot(
            low[:, :ADAPTER_RANK], key_up_ref[...].astype(jnp.bfloat16)
        )
        value_add = adapter_multiplier * dot(
            low[:, ADAPTER_RANK:], value_up_ref[...].astype(jnp.bfloat16)
        )
        cosine = cos_ref[...]
        sine = sin_ref[...]
        width = KEY_VALUE_HEADS * HEAD_DIMENSION
        for head in range(KEY_VALUE_HEADS):
            span = slice(head * HEAD_DIMENSION, (head + 1) * HEAD_DIMENSION)
            linear = acc[:, span] + key_add[:, span]
            turned = linear * cosine + pltpu.roll(linear, HEAD_DIMENSION // 2, 1) * sine
            kv_ref[2 * head] = turned.astype(jnp.bfloat16)
            kv_ref[2 * head + 1] = (
                acc[:, width + head * HEAD_DIMENSION : width + (head + 1) * HEAD_DIMENSION]
                + value_add[:, span]
            ).astype(jnp.bfloat16)


def project(hidden, codes, absmax, table, perm, down, key_up, value_up, cosine, sine):
    rows, width = hidden.shape
    columns = codes.shape[1]
    steps = codes.shape[0] // CHUNK
    blocks = absmax.shape[0] // steps
    whole = lambda array: pl.BlockSpec(array.shape, lambda i: (0,) * array.ndim)
    return pl.pallas_call(
        project_kernel,
        grid=(steps,),
        in_specs=[
            pl.BlockSpec((rows, 4 * CHUNK), lambda i: (0, i)),
            pl.BlockSpec((CHUNK, columns), lambda i: (i, 0)),
            pl.BlockSpec((blocks, columns), lambda i: (i, 0)),
            whole(table),
            whole(perm),
            pl.BlockSpec((2 * ADAPTER_RANK, 4 * CHUNK), lambda i: (0, i)),
            whole(key_up),
            whole(value_up),
            whole(cosine),
            whole(sine),
        ],
        out_specs=[
            pl.BlockSpec((4 * CHUNK, columns), lambda i: (i, 0)),
            pl.BlockSpec((4 * CHUNK, rows), lambda i: (i, 0)),
            pl.BlockSpec((2 * KEY_VALUE_HEADS, rows, HEAD_DIMENSION), lambda i: (0, 0, 0)),
            pl.BlockSpec((rows, 2 * ADAPTER_RANK), lambda i: (0, 0)),
        ],
        out_shape=[
            jax.ShapeDtypeStruct((width, columns), jnp.bfloat16),
            jax.ShapeDtypeStruct((width, rows), jnp.bfloat16),
            jax.ShapeDtypeStruct((2 * KEY_VALUE_HEADS, rows, HEAD_DIMENSION), jnp.bfloat16),
            jax.ShapeDtypeStruct((rows, 2 * ADAPTER_RANK), jnp.bfloat16),
        ],
        scratch_shapes=[
            pltpu.VMEM((rows, columns), jnp.float32),
            pltpu.VMEM((rows, 2 * ADAPTER_RANK), jnp.float32),
        ],
        compiler_params=pltpu.CompilerParams(vmem_limit_bytes=40 * 1024 * 1024),
        cost_estimate=pl.CostEstimate(
            flops=16 * rows * width * columns,
            bytes_accessed=4 * codes.size + 2 * width * columns,
            transcendentals=0,
        ),
    )(hidden, codes, absmax, table, perm, down, key_up, value_up, cosine, sine)


def attention_kernel(
    parts,
    row_block,
    scalars,
    qg_ref,
    own_ref,
    other_ref,
    back_ref,
    keep_ref,
    send_ref,
    keys,
    values,
    keys_t,
    values_t,
    key_grad,
    value_grad,
    cap_scr,
    weight_scr,
):
    step = pl.program_id(0)
    token_count = keys.shape[0]
    prompt_rows = 3 * token_count // 4
    reply_rows = token_count // 8
    sub_rows = row_block // parts
    even = scalars[3] == 0
    prompt_length = scalars[0]

    @pl.when(step == 0)
    def _():
        own = own_ref[...]
        other = other_ref[...]
        key = jnp.where(even, own.astype(jnp.float32), other.astype(jnp.float32))
        value = jnp.where(even, other.astype(jnp.float32), own.astype(jnp.float32))
        keys[...] = key.astype(jnp.bfloat16)
        values[...] = value.astype(jnp.bfloat16)
        keys_t[...] = jnp.transpose(key).astype(jnp.bfloat16)
        values_t[...] = jnp.transpose(value).astype(jnp.bfloat16)
        key_grad[...] = jnp.zeros_like(key_grad)
        value_grad[...] = jnp.zeros_like(value_grad)

    count = BLOCK_Q // sub_rows
    query = jnp.concatenate([qg_ref[s, :sub_rows] for s in range(count)], axis=0)
    grad = jnp.concatenate([qg_ref[s, sub_rows:] for s in range(count)], axis=0)

    lane = lax.broadcasted_iota(jnp.int32, (1, BLOCK_Q), 1)
    span = BLOCK_Q * parts
    first_row = step * span
    query_row = first_row + (lane // sub_rows) * row_block + scalars[4] * sub_rows + lane % sub_rows
    in_prompt = first_row < prompt_rows
    in_chosen = first_row < prompt_rows + reply_rows
    segment_start = jnp.where(
        in_prompt, 0, jnp.where(in_chosen, prompt_rows, prompt_rows + reply_rows)
    )
    segment_length = jnp.where(in_prompt, scalars[0], jnp.where(in_chosen, scalars[1], scalars[2]))
    valid = query_row - segment_start < segment_length
    query_limit = jnp.where(valid, query_row, -1)
    any_valid = first_row - segment_start < segment_length
    prompt_blocks = (prompt_length + BLOCK_K - 1) // BLOCK_K
    prompt_count = jnp.where(
        in_prompt, jnp.minimum(prompt_blocks, (first_row + span) // BLOCK_K), prompt_blocks
    )
    reply_count = jnp.where(
        in_prompt,
        0,
        jnp.minimum(
            (segment_length + BLOCK_K - 1) // BLOCK_K,
            (first_row + span - segment_start) // BLOCK_K,
        ),
    )
    prompt_count = jnp.where(any_valid, prompt_count, 0)
    total_count = jnp.where(any_valid, prompt_count + reply_count, 0)
    reply_base = segment_start // BLOCK_K - prompt_count

    def block_start(j):
        index = jnp.where(j < prompt_count, j, j + reply_base)
        return pl.multiple_of(index * BLOCK_K, BLOCK_K)

    key_iota = lax.broadcasted_iota(jnp.int32, (BLOCK_K, BLOCK_Q), 0)

    def forward(j, carry):
        numerator, total = carry
        start = block_start(j)
        slot = pl.multiple_of(j * BLOCK_K, BLOCK_K)
        key_end = jnp.where(j < prompt_count, prompt_length, segment_start + segment_length)
        threshold = jnp.minimum(query_limit, key_end - 1) - start
        raw = dot(keys[pl.ds(start, BLOCK_K), :], query, NT)
        cap = jnp.tanh(raw * (score_scale / soft_cap))
        weights = jnp.where(key_iota <= threshold, jnp.exp(cap * soft_cap), 0.0)
        cap_scr[pl.ds(slot, BLOCK_K), :] = cap
        weight_scr[pl.ds(slot, BLOCK_K), :] = weights
        numerator = numerator + dot(
            values_t[:, pl.ds(start, BLOCK_K)], weights.astype(jnp.bfloat16)
        )
        total = total + jnp.sum(weights, axis=0, keepdims=True)
        return numerator, total

    numerator, total = lax.fori_loop(
        0,
        total_count,
        forward,
        (
            jnp.zeros((HEAD_DIMENSION, BLOCK_Q), jnp.float32),
            jnp.zeros((1, BLOCK_Q), jnp.float32),
        ),
    )
    denominator = total + jnp.where(valid, 0.0, 1.0)
    inverse = 1.0 / denominator
    output = (numerator / denominator).astype(jnp.bfloat16).astype(jnp.float32)
    delta = jnp.sum(output * jnp.transpose(grad.astype(jnp.float32)), axis=0, keepdims=True)

    def backward(j, query_grad):
        start = block_start(j)
        slot = pl.multiple_of(j * BLOCK_K, BLOCK_K)
        cap = cap_scr[pl.ds(slot, BLOCK_K), :]
        prob = weight_scr[pl.ds(slot, BLOCK_K), :] * inverse
        grad_prob = dot(values[pl.ds(start, BLOCK_K), :], grad, NT)
        slope = (
            prob * (grad_prob - delta) * (score_scale - score_scale * cap * cap)
        ).astype(jnp.bfloat16)
        key_grad[pl.ds(start, BLOCK_K), :] += dot(slope, query)
        value_grad[pl.ds(start, BLOCK_K), :] += dot(prob.astype(jnp.bfloat16), grad)
        return query_grad + dot(keys_t[:, pl.ds(start, BLOCK_K)], slope)

    query_grad = lax.fori_loop(
        0, total_count, backward, jnp.zeros((HEAD_DIMENSION, BLOCK_Q), jnp.float32)
    )
    output_rows = jnp.transpose(output).astype(jnp.bfloat16)
    grad_rows = jnp.transpose(query_grad).astype(jnp.bfloat16)
    for s in range(count):
        back_ref[s, :sub_rows] = output_rows[s * sub_rows : (s + 1) * sub_rows]
        back_ref[s, sub_rows:] = grad_rows[s * sub_rows : (s + 1) * sub_rows]

    @pl.when(step == pl.num_programs(0) - 1)
    def _():
        keep_ref[...] = jnp.where(even, key_grad[...], value_grad[...])
        send_ref[...] = jnp.where(even, value_grad[...], key_grad[...])


def attention(scalars, received, own, other, parts, row_block):
    token_count = own.shape[0]
    sub_rows = row_block // parts
    count = BLOCK_Q // sub_rows
    steps = received.shape[0] // count
    whole = lambda: pl.BlockSpec((token_count, HEAD_DIMENSION), lambda i: (0, 0))
    pairs = token_count * token_count // parts
    return pl.pallas_call(
        functools.partial(attention_kernel, parts, row_block),
        grid=(steps,),
        in_specs=[
            pl.BlockSpec(memory_space=pltpu.SMEM),
            pl.BlockSpec((count, 2 * sub_rows, HEAD_DIMENSION), lambda i: (i, 0, 0)),
            whole(),
            whole(),
        ],
        out_specs=[
            pl.BlockSpec((count, 2 * sub_rows, HEAD_DIMENSION), lambda i: (i, 0, 0)),
            whole(),
            whole(),
        ],
        out_shape=[
            jax.ShapeDtypeStruct(received.shape, jnp.bfloat16),
            jax.ShapeDtypeStruct((token_count, HEAD_DIMENSION), jnp.float32),
            jax.ShapeDtypeStruct((token_count, HEAD_DIMENSION), jnp.float32),
        ],
        scratch_shapes=[
            pltpu.VMEM((token_count, HEAD_DIMENSION), jnp.bfloat16),
            pltpu.VMEM((token_count, HEAD_DIMENSION), jnp.bfloat16),
            pltpu.VMEM((HEAD_DIMENSION, token_count), jnp.bfloat16),
            pltpu.VMEM((HEAD_DIMENSION, token_count), jnp.bfloat16),
            pltpu.VMEM((token_count, HEAD_DIMENSION), jnp.float32),
            pltpu.VMEM((token_count, HEAD_DIMENSION), jnp.float32),
            pltpu.VMEM((token_count, BLOCK_Q), jnp.float32),
            pltpu.VMEM((token_count, BLOCK_Q), jnp.float32),
        ],
        compiler_params=pltpu.CompilerParams(vmem_limit_bytes=48 * 1024 * 1024),
        cost_estimate=pl.CostEstimate(
            flops=60 * pairs * HEAD_DIMENSION, bytes_accessed=8 * own.size, transcendentals=pairs
        ),
    )(scalars, received, own, other)


def input_grad_kernel(grad_ref, weight_ref, low_ref, down_ref, perm_ref, out_ref):
    perm = perm_ref[...]
    down = dot(down_ref[...].astype(jnp.bfloat16), perm).astype(jnp.bfloat16)
    mixed = dot(grad_ref[...], weight_ref[...], NT) + dot(low_ref[...], down)
    out_ref[...] = dot(mixed.astype(jnp.bfloat16), perm, NT).astype(jnp.bfloat16)


def input_grad(grad, weight, low, down, perm):
    rows = grad.shape[0]
    width, columns = weight.shape
    whole = lambda array: pl.BlockSpec(array.shape, lambda i: (0,) * array.ndim)
    return pl.pallas_call(
        input_grad_kernel,
        grid=(width // (4 * CHUNK),),
        in_specs=[
            whole(grad),
            pl.BlockSpec((4 * CHUNK, columns), lambda i: (i, 0)),
            whole(low),
            pl.BlockSpec((low.shape[1], 4 * CHUNK), lambda i: (0, i)),
            whole(perm),
        ],
        out_specs=pl.BlockSpec((rows, 4 * CHUNK), lambda i: (0, i)),
        out_shape=jax.ShapeDtypeStruct((rows, width), jnp.bfloat16),
        compiler_params=pltpu.CompilerParams(vmem_limit_bytes=40 * 1024 * 1024),
        cost_estimate=pl.CostEstimate(
            flops=8 * rows * width * columns, bytes_accessed=2 * width * columns, transcendentals=0
        ),
    )(grad, weight, low, down, perm)


def gather_heads_kernel(parts, scalars, query_ref, chosen_ref, rejected_ref, out_ref):
    rows = query_ref.shape[0]
    sub_rows = rows // parts
    for part in range(parts):
        span = slice(part * sub_rows, (part + 1) * sub_rows)
        for head in range(HEADS):
            place = (head // 2 * parts + part) * 2 + head % 2
            lanes = slice(head * HEAD_DIMENSION, (head + 1) * HEAD_DIMENSION)
            out_ref[place, :sub_rows] = query_ref[span, lanes]
            out_ref[place, sub_rows:] = (
                scalars[0]
                * (
                    rejected_ref[span, lanes].astype(jnp.float32) * scalars[2]
                    - chosen_ref[span, lanes].astype(jnp.float32) * scalars[1]
                )
            ).astype(jnp.bfloat16)


def gather_heads(scalars, queries, chosen, rejected, parts):
    rows, width = queries.shape
    return pl.pallas_call(
        functools.partial(gather_heads_kernel, parts),
        in_specs=[pl.BlockSpec(memory_space=pltpu.SMEM)]
        + [pl.BlockSpec(memory_space=pltpu.VMEM)] * 3,
        out_specs=pl.BlockSpec(memory_space=pltpu.VMEM),
        out_shape=jax.ShapeDtypeStruct(
            (HEADS * parts, 2 * rows // parts, HEAD_DIMENSION), jnp.bfloat16
        ),
        compiler_params=pltpu.CompilerParams(vmem_limit_bytes=16 * 1024 * 1024),
    )(scalars, queries, chosen, rejected)


def scatter_heads_kernel(parts, back_ref, output_ref, grad_ref):
    sub_rows = output_ref.shape[0] // parts
    for part in range(parts):
        span = slice(part * sub_rows, (part + 1) * sub_rows)
        for head in range(HEADS):
            place = (head // 2 * parts + part) * 2 + head % 2
            lanes = slice(head * HEAD_DIMENSION, (head + 1) * HEAD_DIMENSION)
            output_ref[span, lanes] = back_ref[place, :sub_rows]
            grad_ref[span, lanes] = back_ref[place, sub_rows : 2 * sub_rows]


def scatter_heads(back, parts, rows):
    shape = jax.ShapeDtypeStruct((rows, HEADS * HEAD_DIMENSION), jnp.bfloat16)
    return pl.pallas_call(
        functools.partial(scatter_heads_kernel, parts),
        in_specs=[pl.BlockSpec(memory_space=pltpu.VMEM)],
        out_specs=[pl.BlockSpec(memory_space=pltpu.VMEM)] * 2,
        out_shape=[shape, shape],
        compiler_params=pltpu.CompilerParams(vmem_limit_bytes=16 * 1024 * 1024),
    )(back)


def rope_tables(lengths, token_count):
    small = 64
    prompt_rows = 3 * token_count // 4
    reply_rows = token_count // 8
    start = jnp.arange(token_count // small, dtype=jnp.int32) * small
    position = jnp.where(
        start < prompt_rows, start, lengths[0] + lax.rem(start - prompt_rows, reply_rows)
    )
    half = HEAD_DIMENSION // 2
    inverse = rope_base ** (-2.0 * jnp.arange(half, dtype=jnp.float32) / HEAD_DIMENSION)
    large = position.astype(jnp.float32)[:, None] * inverse[None, :]
    little = jnp.arange(small, dtype=jnp.float32)[:, None] * inverse[None, :]
    double = lambda array: jnp.concatenate([array, array], axis=1)
    large_cos, large_sin = double(jnp.cos(large))[:, None], double(jnp.sin(large))[:, None]
    little_cos, little_sin = double(jnp.cos(little))[None], double(jnp.sin(little))[None]
    cosine = large_cos * little_cos - large_sin * little_sin
    sine = large_sin * little_cos + large_cos * little_sin
    sign = jnp.where(jnp.arange(HEAD_DIMENSION) < half, -1.0, 1.0).astype(jnp.float32)
    shape = (token_count, HEAD_DIMENSION)
    return cosine.reshape(shape), (sine * sign).reshape(shape)


def per_device(
    hidden,
    packed_weight_codes,
    block_scale_codes,
    grouped_scale,
    adapter_down_weight,
    key_up_weight,
    value_up_weight,
    queries,
    chosen_output_gradient,
    rejected_output_gradient,
    sequence_log_likelihoods,
    lengths,
):
    rows_here, width = hidden.shape
    seq_count = lax.axis_size("seq")
    me = lax.axis_index("seq")
    token_count = rows_here * seq_count
    prompt_rows = 3 * token_count // 4
    reply_rows = token_count // 8
    parts = seq_count // HEADS
    sub_rows = rows_here // parts
    parity = lax.rem(me, 2)
    part = lax.rem(me // 2, parts)

    margin = dpo_beta * (
        sequence_log_likelihoods[0]
        - sequence_log_likelihoods[2]
        - (sequence_log_likelihoods[1] - sequence_log_likelihoods[3])
    )
    pair_weight = dpo_beta * jax.nn.sigmoid(-margin)
    first_row = me * rows_here
    in_chosen = jnp.where(first_row < prompt_rows + reply_rows, 1.0, 0.0)
    in_rejected = jnp.where(
        (first_row < prompt_rows) | (first_row >= prompt_rows + reply_rows), 1.0, 0.0
    )

    def exchange(array):
        return lax.all_to_all(array, "seq", split_axis=0, concat_axis=0, tiled=True)

    def swap(array):
        return lax.ppermute(array, "seq", [(i, i ^ 1) for i in range(seq_count)])

    sent = gather_heads(
        jnp.stack([pair_weight, in_chosen, in_rejected]),
        queries,
        chosen_output_gradient,
        rejected_output_gradient,
        parts,
    )
    sent, codes = lax.optimization_barrier((sent, packed_weight_codes))
    received = exchange(sent)

    cosine, sine = rope_tables(lengths, token_count)
    own_cosine = lax.dynamic_slice_in_dim(cosine, me * rows_here, rows_here, 0)
    own_sine = lax.dynamic_slice_in_dim(sine, me * rows_here, rows_here, 0)
    columns = packed_weight_codes.shape[1]
    group_count = grouped_scale.shape[1]
    spread = jnp.repeat(grouped_scale, columns // group_count, axis=1)
    absmax = spread * (block_scale_codes.astype(jnp.float32) + 1.0) / 256.0
    table = jnp.zeros((CHUNK, 128), jnp.float32) + jnp.pad(
        jnp.array(nf4_levels, jnp.float32), (0, 112)
    )
    source = jnp.arange(4 * CHUNK)
    perm = (source[:, None] == (4 * (source % CHUNK) + source // CHUNK)[None, :]).astype(
        jnp.bfloat16
    )
    weight, hidden_t, kv, low_rank = project(
        hidden,
        codes,
        absmax,
        table,
        perm,
        adapter_down_weight,
        key_up_weight,
        value_up_weight,
        own_cosine,
        own_sine,
    )
    if parts > 1:
        kv = jnp.broadcast_to(
            kv.reshape(KEY_VALUE_HEADS, 1, 2, rows_here, HEAD_DIMENSION),
            (KEY_VALUE_HEADS, parts, 2, rows_here, HEAD_DIMENSION),
        ).reshape(seq_count, rows_here, HEAD_DIMENSION)
    kv, received = lax.optimization_barrier((kv, received))
    own = exchange(kv).reshape(token_count, HEAD_DIMENSION)
    other = swap(own)
    low_halves = jnp.transpose(low_rank).reshape(1, 2, ADAPTER_RANK, rows_here)
    early = jnp.concatenate(
        [
            hidden_t.reshape(seq_count, width // seq_count, rows_here),
            jnp.broadcast_to(
                low_halves, (seq_count // 2, 2, ADAPTER_RANK, rows_here)
            ).reshape(seq_count, ADAPTER_RANK, rows_here),
        ],
        axis=1,
    )
    early, other = lax.optimization_barrier((early, other))
    early = exchange(early)

    scalars = jnp.concatenate([lengths, jnp.stack([parity, part]).astype(jnp.int32)])
    back, keep, send = attention(scalars, received, own, other, parts, rows_here)
    send, early = lax.optimization_barrier((send, early))
    total = keep + swap(send)
    if parts > 1:
        groups = [
            [2 * parts * h + 2 * r + c for r in range(parts)]
            for h in range(KEY_VALUE_HEADS)
            for c in range(2)
        ]
        total = lax.psum(total, "seq", axis_index_groups=groups)
    half = HEAD_DIMENSION // 2
    turned = total * cosine - jnp.roll(total, half, axis=1) * sine
    grad_column = jnp.where(parity == 0, turned, total).astype(jnp.bfloat16)
    slice_rows = width // seq_count
    early = jnp.transpose(early, (1, 0, 2)).reshape(slice_rows + ADAPTER_RANK, token_count)
    up_grad = adapter_multiplier * dot(early[slice_rows:], grad_column)
    gathered = exchange(grad_column.reshape(seq_count, rows_here, HEAD_DIMENSION))
    pieces = gathered.reshape(KEY_VALUE_HEADS, parts, 2, rows_here, HEAD_DIMENSION)[:, 0]
    projection_gradient = jnp.transpose(pieces, (2, 1, 0, 3)).reshape(rows_here, -1)
    key_width = KEY_VALUE_HEADS * HEAD_DIMENSION
    low_gradient = (
        adapter_multiplier
        * jnp.concatenate(
            [
                dot(projection_gradient[:, :key_width], key_up_weight.astype(jnp.bfloat16), NT),
                dot(projection_gradient[:, key_width:], value_up_weight.astype(jnp.bfloat16), NT),
            ],
            axis=1,
        )
    ).astype(jnp.bfloat16)
    late = exchange(
        jnp.concatenate(
            [back, jnp.broadcast_to(low_gradient[None], (seq_count, rows_here, 2 * ADAPTER_RANK))],
            axis=1,
        )
    )
    hidden_gradient = input_grad(
        projection_gradient, weight, low_gradient, adapter_down_weight, perm
    )
    late, hidden_gradient = lax.optimization_barrier((late, hidden_gradient))
    low_gradient_all = late[:, 2 * sub_rows :]
    down_slice = dot(
        early[:slice_rows], low_gradient_all.reshape(token_count, 2 * ADAPTER_RANK)
    )
    finals = lax.all_gather(
        jnp.concatenate([down_slice, up_grad], axis=0).astype(jnp.bfloat16), "seq", axis=0
    )
    adapter_down_gradient = jnp.transpose(
        finals[:, :slice_rows].reshape(width, 2 * ADAPTER_RANK)
    ).astype(jnp.float32)
    ups = finals[:, slice_rows:].reshape(
        KEY_VALUE_HEADS, parts, 2, ADAPTER_RANK, HEAD_DIMENSION
    )[:, 0]
    ups = jnp.transpose(ups, (1, 2, 0, 3)).reshape(2, ADAPTER_RANK, key_width).astype(jnp.float32)

    attention_output, query_gradient = scatter_heads(late, parts, rows_here)
    return (
        attention_output,
        query_gradient,
        hidden_gradient,
        adapter_down_gradient,
        ups[0],
        ups[1],
    )


def solution(mesh):
    rows = P(("groups", "seq"), None)
    in_specs = (rows,) + (P(),) * 6 + (rows,) * 3 + (P("groups"),) * 2
    out_specs = (rows,) * 3 + (P("groups", None),) * 3
    return jax.shard_map(
        per_device, mesh=mesh, in_specs=in_specs, out_specs=out_specs, check_vma=False
    )
```
